256 devices in a mesh: ctx: 32 (over z, y_lo, core), head: 8 (over y_hi, x).
Axes of the slice: x: 4, y: 4 (y_hi: 2, y_lo: 2; y = y_hi * 2 + y_lo), z: 8, core: 2. Of those that a mesh axis runs over, the one named last changes fastest.
Arguments:
- queries: bfloat16 [2048, 64, 576], P('ctx', 'head'), may hold values from -4.5 to 4.5
- latent: bfloat16 [2048, 576], P('ctx'), may hold values from -5 to 5
- grad_out: bfloat16 [2048, 64, 512], P('ctx', 'head'), may hold values from -1.1953125 to 1.1953125
- block_order: int32 [64], replicated, may hold values from 0 to 63, each once
Outputs:
- grad_queries: bfloat16 [2048, 64, 576], P('ctx', 'head')
- grad_latent: float32 [2048, 576], P(('ctx', 'head'))
The draws below stay inside these ranges and needn't reach their ends.
All inputs are finite; a program needn't handle non-finite values.
Results may differ from the reference program's by a relative error of at most 0.0045.
Values may be sent and summed in bfloat16 or wider, within the bound.
No kernel may reach another device: no remote copies, remote signals or barrier semaphores. Data moves between devices by JAX's collectives and lax.ppermute only.
A program may use at most 64 MiB of HBM per device.

```python
import jax
import jax.numpy as jnp
from jax import lax

KV_RANK = 512
ROPE = 64
TOK_DEV = 64
HEADS = 64
TOKENS = 2048
N_CTX = 32


def draw_queries(key, part):
    shape = (TOKENS, HEADS, KV_RANK + ROPE)
    base = 0.6 * jnp.clip(jax.random.normal(jax.random.fold_in(key, 13), shape, jnp.float32), -6.0, 6.0)
    return base.astype(jnp.bfloat16)


def draw_latent(key, part):
    shape = (TOKENS, KV_RANK + ROPE)
    base = jax.random.normal(jax.random.fold_in(key, 21), shape, jnp.float32)
    base = jnp.clip(base, -5.0, 5.0)
    return base.astype(jnp.bfloat16)


def block_scale(own_key, extent, shards, smallest, largest):
    level, own = 1.0, jax.random.fold_in(own_key, 6)
    for position, parts in shards:
        steps = jnp.exp(jax.random.uniform(jax.random.fold_in(own, position), (parts,), jnp.float32, smallest / len(shards), largest / len(shards)))
        level = level * jnp.repeat(steps, extent[position] // parts).reshape([-1 if axis == position else 1 for axis in range(len(extent))])
    return level


def noise(rng, shape, width, limit, shards=(), kind=jnp.bfloat16):
    array = width * jax.random.normal(rng, shape, jnp.float32)
    if shards:
        array = array * block_scale(rng, shape, shards, -0.22, 0.18)
    return jnp.clip(array, -limit, limit).astype(kind)


def setup_inputs(seed: int = 0) -> dict:
    seeds = jax.random.split(jax.random.key(seed), 5)
    return {
        "queries": draw_queries(jax.random.fold_in(seeds[4], 71), 0),
        "latent": draw_latent(jax.random.fold_in(seeds[4], 71), 0),
        "grad_out": noise(seeds[2], (TOKENS, HEADS, KV_RANK), 0.2, 1.1953125, ((0, 32), (1, 8))),
        "block_order": jax.random.permutation(seeds[3], 2 * N_CTX).astype(jnp.int32),
    }


score_scale = 192.0 ** -0.5
masked_low = -1.0e30


def reference(queries, latent, grad_out, block_order):
    half_rows = TOK_DEV // 2
    row_ids = jnp.arange(TOKENS, dtype=jnp.int32)
    positions = block_order[row_ids // half_rows] * half_rows + row_ids % half_rows
    visible = positions[None, :] <= positions[:, None]
    values = latent[:, :KV_RANK]

    def per_head(grad_sum, head_id):
        query_h = lax.dynamic_index_in_dim(queries, head_id, 1, keepdims=False)
        grad_h = lax.dynamic_index_in_dim(grad_out, head_id, 1, keepdims=False)
        scores = jnp.dot(query_h, latent.T, preferred_element_type=jnp.float32) * score_scale
        scores = jnp.where(visible, scores, masked_low)
        row_max = jnp.max(scores, axis=1, keepdims=True)
        summed = jnp.sum(jnp.where(visible, jnp.exp(scores - row_max), 0.0), axis=1, keepdims=True)
        log_norm = row_max + jnp.log(summed)
        attention = jnp.where(visible, jnp.exp(scores - log_norm), 0.0)
        value_prod = jnp.dot(grad_h, values.T, preferred_element_type=jnp.float32)
        row_delta = jnp.sum(attention * value_prod, axis=1, keepdims=True)
        score_grad = (score_scale * attention * (value_prod - row_delta)).astype(jnp.bfloat16)
        weights = attention.astype(jnp.bfloat16)
        grad_query = jnp.dot(score_grad, latent, preferred_element_type=jnp.float32).astype(jnp.bfloat16)
        key_term = jnp.dot(score_grad.T, query_h, preferred_element_type=jnp.float32)
        value_term = jnp.dot(weights.T, grad_h, preferred_element_type=jnp.float32)
        key_term = key_term + jnp.pad(value_term, ((0, 0), (0, ROPE)))
        return grad_sum + key_term, grad_query

    start_sum = jnp.zeros((TOKENS, KV_RANK + ROPE), jnp.float32)
    grad_latent, grad_stack = lax.scan(per_head, start_sum, jnp.arange(HEADS, dtype=jnp.int32))
    return jnp.transpose(grad_stack, (1, 0, 2)), grad_latent
```

```python
import jax
import jax.numpy as jnp
from jax import lax
from jax.experimental import pallas as pl
from jax.experimental.pallas import tpu as pltpu
from jax.sharding import Mesh, PartitionSpec as P

CTX = ("z", "yl", "c")
HEAD = ("yh", "x")
KV_RANK = 512
WIDTH = 576
SCALE = 192.0 ** (-0.5)
LOW = -1e30
CHUNK = 256
KEYS = 2048
ROWS = 512


def nn(a, b):
    return lax.dot_general(a, b, (((1,), (0,)), ((), ())), preferred_element_type=jnp.float32)


def nt(a, b):
    return lax.dot_general(a, b, (((1,), (1,)), ((), ())), preferred_element_type=jnp.float32)


def tn(a, b):
    return lax.dot_general(a, b, (((0,), (0,)), ((), ())), preferred_element_type=jnp.float32)


def attention_kernel(
    order_ref, where_ref, own_ref, other_ref, q_ref, g_ref,
    dq_ref, own_out, other_out,
    p_scr, vp_scr, ds_scr, stat_scr,
):
    ctx, core = where_ref[0], where_ref[1]
    lane = lax.broadcasted_iota(jnp.int32, (1, ROWS), 1)
    tok = lane // 8
    query_pos = jnp.where(
        tok < 32, order_ref[2 * ctx] * 32 + tok, order_ref[2 * ctx + 1] * 32 + tok - 32
    )
    sub = lax.broadcasted_iota(jnp.int32, (8, 128), 0)
    q = q_ref[...]
    g = g_ref[...]
    n_chunks = KEYS // CHUNK
    half_chunks = n_chunks // 2

    running_max = jnp.full((1, ROWS), LOW, jnp.float32)
    total = jnp.zeros((1, ROWS), jnp.float32)
    weighted = jnp.zeros((1, ROWS), jnp.float32)
    for i in range(n_chunks):
        k_ref = own_ref if i < half_chunks else other_ref
        base = (i % half_chunks) * CHUNK
        key_core = core if i < half_chunks else 1 - core
        keys = k_ref[base:base + CHUNK, :]
        tiles = []
        for t in range(CHUNK // 8):
            u = base // 8 + t
            z, piece = u % 8, u // 8
            yl, yh, x = piece // 8, (piece // 4) % 2, piece % 4
            block = ((z * 2 + yl) * 2 + key_core) * 2 + yh
            tiles.append(sub + (order_ref[block] * 32 + x * 8))
        key_pos = jnp.concatenate(tiles, axis=0)
        key_pos = jnp.concatenate([key_pos] * (ROWS // 128), axis=1)
        visible = key_pos <= query_pos
        scores = jnp.where(visible, nt(keys, q) * SCALE, LOW)
        value_prod = nt(keys[:, :KV_RANK], g)
        new_max = jnp.maximum(running_max, jnp.max(scores, axis=0, keepdims=True))
        carry = jnp.exp(running_max - new_max)
        p = jnp.where(visible, jnp.exp(scores - new_max), 0.0)
        total = total * carry + jnp.sum(p, axis=0, keepdims=True)
        weighted = weighted * carry + jnp.sum(p * value_prod, axis=0, keepdims=True)
        running_max = new_max
        p_scr[i * CHUNK:(i + 1) * CHUNK, :] = p
        vp_scr[i * CHUNK:(i + 1) * CHUNK, :] = value_prod
        stat_scr[i:i + 1, :] = new_max
    inv = 1.0 / total
    delta = weighted * inv
    for i in range(n_chunks):
        out_ref = own_out if i < half_chunks else other_out
        base = (i % half_chunks) * CHUNK
        factor = jnp.exp(stat_scr[i:i + 1, :] - running_max) * inv
        attention = p_scr[i * CHUNK:(i + 1) * CHUNK, :] * factor
        ds = (SCALE * attention * (vp_scr[i * CHUNK:(i + 1) * CHUNK, :] - delta)).astype(jnp.bfloat16)
        w = attention.astype(jnp.bfloat16)
        ds_scr[i * CHUNK:(i + 1) * CHUNK, :] = ds
        out_ref[base:base + CHUNK, :KV_RANK] = (nn(ds, q[:, :KV_RANK]) + nn(w, g)).astype(out_ref.dtype)
        out_ref[base:base + CHUNK, KV_RANK:] = nn(ds, q[:, KV_RANK:]).astype(out_ref.dtype)
    half = KEYS // 2
    dq_ref[...] = (
        tn(ds_scr[:half, :], own_ref[...]) + tn(ds_scr[half:, :], other_ref[...])
    ).astype(dq_ref.dtype)


def attention_call(order, where, own, other, q, g):
    half = KEYS // 2
    vmem = pl.BlockSpec(memory_space=pltpu.VMEM)
    smem = pl.BlockSpec(memory_space=pltpu.SMEM)
    return pl.pallas_call(
        attention_kernel,
        out_shape=(
            jax.ShapeDtypeStruct((ROWS, WIDTH), jnp.bfloat16),
            jax.ShapeDtypeStruct((half, WIDTH), jnp.float32),
            jax.ShapeDtypeStruct((half, WIDTH), jnp.bfloat16),
        ),
        in_specs=[smem, smem, vmem, vmem, vmem, vmem],
        out_specs=(vmem, vmem, vmem),
        scratch_shapes=[
            pltpu.VMEM((KEYS, ROWS), jnp.float32),
            pltpu.VMEM((KEYS, ROWS), jnp.float32),
            pltpu.VMEM((KEYS, ROWS), jnp.bfloat16),
            pltpu.VMEM((8, ROWS), jnp.float32),
        ],
        compiler_params=pltpu.CompilerParams(vmem_limit_bytes=48 * 2**20),
        cost_estimate=pl.CostEstimate(
            flops=2 * KEYS * ROWS * (3 * WIDTH + 2 * KV_RANK),
            bytes_accessed=10 * 2**20, transcendentals=KEYS * ROWS,
        ),
        name="attention",
    )(order, where, own, other, q, g)


def shards(queries, latent, grad_out, block_order):
    tok_rows, head_count, width = queries.shape
    q = queries.reshape(tok_rows * head_count, width)
    g = grad_out.reshape(tok_rows * head_count, KV_RANK)
    core = lax.axis_index("c")
    where = jnp.stack([lax.axis_index(CTX), core]).astype(jnp.int32)
    piece = lax.dynamic_slice_in_dim(latent, lax.axis_index(HEAD) * 8, 8, 0)
    column = lax.all_to_all(
        jnp.broadcast_to(piece[None], (8, 8, width)), "z", 0, 0, tiled=True
    ).reshape(64, width)
    own = lax.all_to_all(
        jnp.broadcast_to(column[None], (16, 64, width)), ("yl", "yh", "x"), 0, 0, tiled=True
    ).reshape(1024, width)
    swap = [(0, 1), (1, 0)]
    other = lax.ppermute(own, "c", swap)
    dq, kept, given = attention_call(block_order, where, own, other, q, g)
    taken = lax.ppermute(given, "c", swap)
    part = (kept + taken.astype(jnp.float32)).astype(jnp.bfloat16)
    part = lax.all_to_all(part.reshape(16, 64, width), ("yl", "yh", "x"), 0, 0, tiled=True)
    part = jnp.sum(part.astype(jnp.float32), axis=0).astype(jnp.bfloat16)
    part = lax.all_to_all(part.reshape(8, 8, width), "z", 0, 0, tiled=True)
    return dq.reshape(tok_rows, head_count, width), jnp.sum(part.astype(jnp.float32), axis=0)


def solution(mesh):
    fine = Mesh(mesh.devices.reshape(8, 2, 2, 2, 4), CTX + HEAD)
    placed = (P(CTX, HEAD, None), P(CTX, None), P(CTX, HEAD, None), P())
    return jax.shard_map(
        shards, mesh=fine, in_specs=placed,
        out_specs=(P(CTX, HEAD, None), P(CTX + HEAD, None)), check_vma=False,
    )
```

```python
import itertools

import jax
import jax.numpy as jnp
from jax import lax
from jax.experimental import pallas as pl
from jax.experimental.pallas import tpu as pltpu
from jax.sharding import Mesh, PartitionSpec as P

SIZES = (8, 2, 2, 2, 4)
CTX = ("z", "yl", "c")
HEAD = ("yh", "x")
ALL = CTX + HEAD
KV_RANK = 512
WIDTH = 576
SENT = 640
SCALE = 192.0 ** (-0.5)
LOW = -1e30
ROWS = 512
PART = 256
bf16, f32 = jnp.bfloat16, jnp.float32
FORWARD = (((0, 0),), ((0, 1), (0, 3)), ((0, 2), (1, 0), (1, 1), (1, 3)), ((1, 2),))
BACKWARD = (((1, 2),), ((0, 2), (1, 1)), ((0, 1), (1, 3)), ((0, 3), (1, 0)), ((0, 0),))


def places():
    return itertools.product(*(range(n) for n in SIZES))


def flat(z, yl, c, yh, x):
    return (((z * 2 + yl) * 2 + c) * 2 + yh) * 4 + x


def first_groups():
    found = {}
    for z, yl, c, yh, x in places():
        found.setdefault((c, x) if c == 0 else (c, yl, yh), []).append(flat(z, yl, c, yh, x))
    return list(found.values())


def turn(value, shift):
    pairs = []
    for z, yl, c, yh, x in places():
        y = 2 * yh + yl
        if c == 0:
            to = flat(z, yl, c, yh, (x + shift) % 4)
        else:
            y = (y + shift) % 4
            to = flat(z, y % 2, c, y // 2, x)
        pairs.append((flat(z, yl, c, yh, x), to))
    return lax.ppermute(value, ALL, pairs)


def swap(value):
    return lax.ppermute(value, "c", [(0, 1), (1, 0)])


def nn(a, b):
    return lax.dot_general(a, b, (((1,), (0,)), ((), ())), preferred_element_type=f32)


def nt(a, b):
    return lax.dot_general(a, b, (((1,), (1,)), ((), ())), preferred_element_type=f32)


def tn(a, b):
    return lax.dot_general(a, b, (((0,), (0,)), ((), ())), preferred_element_type=f32)


def key_positions(order_ref, where_ref, key_core, shift):
    x = lax.rem(where_ref[2] + 4 - shift, 4)
    y = lax.rem(where_ref[3] + 4 - shift, 4)
    yl, yh = lax.rem(y, 2), y // 2
    sub = lax.broadcasted_iota(jnp.int32, (8, 128), 0)
    tiles = []
    for t in range(PART // 8):
        z, a, b = t // 4, (t // 2) % 2, t % 2
        first = ((z * 2 + a) * 2) * 2 + b
        second = ((z * 2 + yl) * 2 + 1) * 2 + yh
        block = jnp.where(key_core == 0, first, second)
        eighth = jnp.where(key_core == 0, x, t % 4)
        tiles.append(sub + (order_ref[block] * 32 + eighth * 8))
    column = jnp.concatenate(tiles, axis=0)
    return jnp.concatenate([column] * (ROWS // 128), axis=1)


def forward_kernel(parts, order_ref, where_ref, stat_ref, *refs):
    n = len(parts)
    key_refs, (q_ref, g_ref), (stat_out, p_out, vp_out) = refs[:n], refs[n:n + 2], refs[n + 2:]
    ctx, core = where_ref[0], where_ref[1]
    tok = lax.broadcasted_iota(jnp.int32, (1, ROWS), 1) // 8
    query_pos = jnp.where(
        tok < 32, order_ref[2 * ctx] * 32 + tok, order_ref[2 * ctx + 1] * 32 + tok - 32
    )
    q, g = q_ref[...], g_ref[...]
    running_max, total, weighted = stat_ref[0:1, :], stat_ref[1:2, :], stat_ref[2:3, :]
    for i, ((half, shift), k_ref) in enumerate(zip(parts, key_refs)):
        key_pos = key_positions(order_ref, where_ref, core if half == 0 else 1 - core, shift)
        visible = key_pos <= query_pos
        scores = jnp.where(visible, nt(k_ref[:, :WIDTH], q) * SCALE, LOW)
        value_prod = nt(k_ref[:, :KV_RANK], g)
        new_max = jnp.maximum(running_max, jnp.max(scores, axis=0, keepdims=True))
        carry = jnp.exp(running_max - new_max)
        p = jnp.where(visible, jnp.exp(scores - new_max), 0.0)
        total = total * carry + jnp.sum(p, axis=0, keepdims=True)
        weighted = weighted * carry + jnp.sum(p * value_prod, axis=0, keepdims=True)
        running_max = new_max
        p_out[i * PART:(i + 1) * PART, :] = p
        vp_out[i * PART:(i + 1) * PART, :] = value_prod
        stat_out[3 + i:4 + i, :] = new_max
    stat_out[0:1, :] = running_max
    stat_out[1:2, :] = total
    stat_out[2:3, :] = weighted


def backward_kernel(parts, last_ref, *refs):
    n = len(parts)
    q, g = refs[3 * n][...], refs[3 * n + 1][...]
    outs = refs[3 * n + 2:]
    inv = 1.0 / last_ref[1:2, :]
    delta = last_ref[2:3, :] * inv
    for i, (place, _) in enumerate(parts):
        stat_ref, p_ref, vp_ref = refs[3 * i:3 * i + 3]
        out_ref, ds_ref = outs[2 * i:2 * i + 2]
        rows = slice(place * PART, (place + 1) * PART)
        factor = jnp.exp(stat_ref[3 + place:4 + place, :] - last_ref[0:1, :]) * inv
        attention = p_ref[rows, :] * factor
        ds = (SCALE * attention * (vp_ref[rows, :] - delta)).astype(bf16)
        ds_ref[...] = ds
        out_ref[:, :KV_RANK] = (nn(ds, q[:, :KV_RANK]) + nn(attention.astype(bf16), g)).astype(out_ref.dtype)
        rope = nn(ds, q[:, KV_RANK:])
        out_ref[:, KV_RANK:] = jnp.concatenate([rope, jnp.zeros_like(rope)], axis=1).astype(out_ref.dtype)


def query_kernel(*refs):
    out = refs[-1]
    ds = jnp.concatenate([r[...] for r in refs[0:-1:2]], axis=0)
    keys = jnp.concatenate([r[:, :WIDTH] for r in refs[1:-1:2]], axis=0)
    out[...] = tn(ds, keys).astype(bf16)


VMEM = pl.BlockSpec(memory_space=pltpu.VMEM)
SMEM = pl.BlockSpec(memory_space=pltpu.SMEM)
LIGHT = pl.CostEstimate(flops=1024, bytes_accessed=1024, transcendentals=0)


def forward_call(parts, order, where, stat, keys, q, g):
    n = len(parts)
    return pl.pallas_call(
        lambda *refs: forward_kernel(parts, *refs),
        out_shape=(
            jax.ShapeDtypeStruct((8, ROWS), f32),
            jax.ShapeDtypeStruct((n * PART, ROWS), f32),
            jax.ShapeDtypeStruct((n * PART, ROWS), f32),
        ),
        in_specs=[SMEM, SMEM] + [VMEM] * (n + 3),
        out_specs=(VMEM,) * 3,
        compiler_params=pltpu.CompilerParams(vmem_limit_bytes=16 * 2**20),
        cost_estimate=LIGHT,
        name="forward_" + "_".join(f"{h}{s}" for h, s in parts),
    )(order, where, stat, *keys, q, g)


def backward_call(wanted, last, saved, q, g):
    parts = [(saved[w][0], w) for w in wanted]
    shapes = []
    for half, _ in wanted:
        shapes.append(jax.ShapeDtypeStruct((PART, SENT), bf16 if half else f32))
        shapes.append(jax.ShapeDtypeStruct((PART, ROWS), bf16))
    out = pl.pallas_call(
        lambda *refs: backward_kernel(parts, *refs),
        out_shape=shapes,
        in_specs=[VMEM] * (3 * len(parts) + 3),
        out_specs=[VMEM] * len(shapes),
        compiler_params=pltpu.CompilerParams(vmem_limit_bytes=16 * 2**20),
        cost_estimate=LIGHT,
        name="backward_" + "_".join(f"{h}{s}" for h, s in wanted),
    )(last, *[a for w in wanted for a in saved[w][1:]], q, g)
    return {w: (out[2 * i], out[2 * i + 1]) for i, w in enumerate(wanted)}


def query_call(pairs):
    return pl.pallas_call(
        query_kernel,
        out_shape=jax.ShapeDtypeStruct((ROWS, WIDTH), bf16),
        in_specs=[VMEM] * (2 * len(pairs)),
        out_specs=VMEM,
        compiler_params=pltpu.CompilerParams(vmem_limit_bytes=16 * 2**20),
        cost_estimate=LIGHT,
        name="query_grad",
    )(*[a for pair in pairs for a in pair])


def shards(queries, latent, grad_out, block_order):
    tok_rows, head_count, width = queries.shape
    q = queries.reshape(tok_rows * head_count, width)
    g = grad_out.reshape(tok_rows * head_count, KV_RANK)
    where = jnp.stack([
        lax.axis_index(CTX), lax.axis_index("c"), lax.axis_index("x"),
        2 * lax.axis_index("yh") + lax.axis_index("yl"),
    ]).astype(jnp.int32)
    groups = first_groups()
    piece = lax.dynamic_slice_in_dim(latent, lax.axis_index(HEAD) * 8, 8, 0)
    piece = jnp.pad(piece, ((0, 0), (0, SENT - WIDTH)))
    first = lax.all_to_all(
        jnp.broadcast_to(piece[None], (32, 8, SENT)), ALL, 0, 0, axis_index_groups=groups, tiled=True
    ).reshape(PART, SENT)
    keys = {(0, 0): first}
    for shift in (1, 3, 2):
        keys[0, shift] = turn(first, shift)
    stat = jnp.concatenate([jnp.full((1, ROWS), LOW, f32), jnp.zeros((7, ROWS), f32)])
    saved = {}
    for wanted in FORWARD:
        for half, shift in wanted:
            if half == 0:
                keys[0, shift], stat = lax.optimization_barrier((keys[0, shift], stat))
                keys[1, shift] = swap(keys[0, shift])
        stat, p, vp = forward_call(wanted, block_order, where, stat, [keys[w] for w in wanted], q, g)
        for i, w in enumerate(wanted):
            saved[w] = (i, stat, p, vp)
    last = stat
    done = {}
    sums = {}
    taken = {}
    for wanted in BACKWARD:
        done.update(backward_call(wanted, last, saved, q, g))
        for half, shift in wanted:
            if half:
                taken[shift] = swap(done[1, shift][0])
        for half, shift in wanted:
            if not half and shift:
                sums[shift] = (done[0, shift][0] + taken[shift].astype(f32)).astype(bf16)
                sums[shift], last = lax.optimization_barrier((sums[shift], last))
    both = done[0, 0][0] + taken[0].astype(f32)
    dq = query_call([(done[w][1], keys[w]) for wanted in BACKWARD for w in wanted])
    arrived = [turn(sums[s], 4 - s) for s in (2, 1, 3)]
    (arrived, dq) = lax.optimization_barrier((arrived, dq))
    arrived = [both] + [a.astype(f32) for a in arrived]
    part = (arrived[0] + arrived[1] + arrived[2] + arrived[3]).astype(bf16)
    part = lax.all_to_all(
        part.reshape(32, 8, SENT), ALL, 0, 0, axis_index_groups=groups, tiled=True
    )
    grad_latent = jnp.sum(part.astype(f32), axis=0)[:, :WIDTH]
    return dq.reshape(tok_rows, head_count, width), grad_latent


def solution(mesh):
    fine = Mesh(mesh.devices.reshape(SIZES), ALL)
    placed = (P(CTX, HEAD, None), P(CTX, None), P(CTX, HEAD, None), P())
    return jax.shard_map(
        shards, mesh=fine, in_specs=placed,
        out_specs=(P(CTX, HEAD, None), P(ALL, None)), check_vma=False,
    )
```

```python
import itertools

import jax
import jax.numpy as jnp
from jax import lax
from jax.experimental import pallas as pl
from jax.experimental.pallas import tpu as pltpu
from jax.sharding import Mesh, PartitionSpec as P

SIZES = (8, 2, 2, 2, 4)
CTX = ("z", "yl", "c")
HEAD = ("yh", "x")
ALL = CTX + HEAD
KV_RANK = 512
WIDTH = 576
SENT = 640
SCALE = 192.0 ** (-0.5)
LOW = -1e30
ROWS = 512
PART = 256
bf16, f32 = jnp.bfloat16, jnp.float32
FORWARD = (((0, 0),), ((0, 1), (0, 3)), ((1, 0), (1, 1), (1, 3)), ((0, 2), (1, 2)))
BACKWARD = (((1, 2),), ((1, 1), (1, 3), (1, 0)), ((0, 2),), ((0, 1), (0, 3)), ((0, 0),))
ORDER = tuple(w for call in FORWARD for w in call)


def places():
    return itertools.product(*(range(n) for n in SIZES))


def flat(z, yl, c, yh, x):
    return (((z * 2 + yl) * 2 + c) * 2 + yh) * 4 + x


def first_groups():
    found = {}
    for z, yl, c, yh, x in places():
        found.setdefault((c, x) if c == 0 else (c, yl, yh), []).append(flat(z, yl, c, yh, x))
    return list(found.values())


def turn(value, shift):
    pairs = []
    for z, yl, c, yh, x in places():
        y = 2 * yh + yl
        if c == 0:
            to = flat(z, yl, c, yh, (x + shift) % 4)
        else:
            y = (y + shift) % 4
            to = flat(z, y % 2, c, y // 2, x)
        pairs.append((flat(z, yl, c, yh, x), to))
    return lax.ppermute(value, ALL, pairs)


def swap(value):
    return lax.ppermute(value, "c", [(0, 1), (1, 0)])


def nn(a, b):
    return lax.dot_general(a, b, (((1,), (0,)), ((), ())), preferred_element_type=f32)


def tn(a, b):
    return lax.dot_general(a, b, (((0,), (0,)), ((), ())), preferred_element_type=f32)


def key_positions(order_ref, where_ref, key_core, shift):
    x = lax.rem(where_ref[2] + 4 - shift, 4)
    y = lax.rem(where_ref[3] + 4 - shift, 4)
    yl, yh = lax.rem(y, 2), y // 2
    sub = lax.broadcasted_iota(jnp.int32, (8, 128), 0)
    tiles = []
    for t in range(PART // 8):
        z, a, b = t // 4, (t // 2) % 2, t % 2
        first = ((z * 2 + a) * 2) * 2 + b
        second = ((z * 2 + yl) * 2 + 1) * 2 + yh
        block = jnp.where(key_core == 0, first, second)
        eighth = jnp.where(key_core == 0, x, t % 4)
        tiles.append(sub + (order_ref[block] * 32 + eighth * 8))
    return jnp.concatenate(tiles, axis=0)


def prepare_kernel(order_ref, where_ref, q_ref, g_ref, q_out, g_out, qt_out, gt_out, key_out, query_out):
    ctx, core = where_ref[0], where_ref[1]
    q, g = q_ref[...], g_ref[...]
    q_out[...] = q
    g_out[...] = g
    qt_out[...] = q.T
    gt_out[...] = g.T
    for i, (half, shift) in enumerate(ORDER):
        key_core = core if half == 0 else 1 - core
        key_out[i * PART:(i + 1) * PART, :] = key_positions(order_ref, where_ref, key_core, shift)
    tok = lax.broadcasted_iota(jnp.int32, (8, ROWS), 1) // 8
    query_out[...] = jnp.where(
        tok < 32, order_ref[2 * ctx] * 32 + tok, order_ref[2 * ctx + 1] * 32 + tok - 32
    )


def load_part(refs, width):
    rows = [r[:, :width] for r in refs]
    return rows[0] if len(rows) == 1 else jnp.concatenate(rows, axis=0)


def forward_kernel(parts, counts, *refs):
    query_pos_ref, key_pos_ref, stat_ref = refs[:3]
    key_refs, at = [], 3
    for count in counts:
        key_refs.append(refs[at:at + count])
        at += count
    qt_ref, gt_ref, stat_out, p_out, vp_out = refs[at:]
    query_pos = query_pos_ref[0:1, :]
    if stat_ref is None:
        running_max = jnp.full((1, ROWS), LOW, f32)
        total = weighted = jnp.zeros((1, ROWS), f32)
    else:
        running_max, total, weighted = stat_ref[0:1, :], stat_ref[1:2, :], stat_ref[2:3, :]
    qt, gt = qt_ref[...], gt_ref[...]
    for i, part in enumerate(parts):
        start = ORDER.index(part) * PART
        key_pos = key_pos_ref[start:start + PART, :]
        key_pos = jnp.concatenate([key_pos] * (ROWS // 128), axis=1)
        visible = key_pos <= query_pos
        scores = jnp.where(visible, nn(load_part(key_refs[i], WIDTH), qt) * SCALE, LOW)
        value_prod = nn(load_part(key_refs[i], KV_RANK), gt)
        new_max = jnp.maximum(running_max, jnp.max(scores, axis=0, keepdims=True))
        carry = jnp.exp(running_max - new_max)
        p = jnp.where(visible, jnp.exp(scores - new_max), 0.0)
        total = total * carry + jnp.sum(p, axis=0, keepdims=True)
        weighted = weighted * carry + jnp.sum(p * value_prod, axis=0, keepdims=True)
        running_max = new_max
        p_out[i * PART:(i + 1) * PART, :] = p
        vp_out[i * PART:(i + 1) * PART, :] = value_prod
        stat_out[3 + i:4 + i, :] = new_max
    stat_out[0:1, :] = running_max
    stat_out[1:2, :] = total
    stat_out[2:3, :] = weighted


def backward_kernel(parts, last_ref, *refs):
    at = sum(4 if added else 3 for _, added in parts)
    q, g = refs[at][...], refs[at + 1][...]
    outs = refs[at + 2:]
    inv = 1.0 / last_ref[1:2, :]
    delta = last_ref[2:3, :] * inv
    at = 0
    for i, (place, added) in enumerate(parts):
        stat_ref, p_ref, vp_ref = refs[at:at + 3]
        out_ref, ds_ref = outs[2 * i:2 * i + 2]
        rows = slice(place * PART, (place + 1) * PART)
        factor = jnp.exp(stat_ref[3 + place:4 + place, :] - last_ref[0:1, :]) * inv
        attention = p_ref[rows, :] * factor
        ds = (SCALE * attention * (vp_ref[rows, :] - delta)).astype(bf16)
        ds_ref[...] = ds
        term = nn(ds, q[:, :KV_RANK]) + nn(attention.astype(bf16), g)
        rope = nn(ds, q[:, KV_RANK:])
        if added:
            term = term + refs[at + 3][:, :KV_RANK].astype(f32)
            rope = rope + refs[at + 3][:, KV_RANK:WIDTH].astype(f32)
        out_ref[:, :KV_RANK] = term.astype(out_ref.dtype)
        out_ref[:, KV_RANK:] = jnp.concatenate([rope, jnp.zeros_like(rope)], axis=1).astype(out_ref.dtype)
        at += 4 if added else 3


def query_kernel(counts, *refs):
    out = refs[-1]
    ds, keys, at = [], [], 0
    for count in counts:
        ds.append(refs[at][...])
        keys.append(load_part(refs[at + 1:at + 1 + count], WIDTH))
        at += 1 + count
    out[...] = tn(jnp.concatenate(ds, axis=0), jnp.concatenate(keys, axis=0)).astype(bf16)


VMEM = pl.BlockSpec(memory_space=pltpu.VMEM)
SMEM = pl.BlockSpec(memory_space=pltpu.SMEM)
LIGHT = pl.CostEstimate(flops=1024, bytes_accessed=1024, transcendentals=0)
PARAMS = pltpu.CompilerParams(vmem_limit_bytes=20 * 2**20)


def call(kernel, name, shapes, smem, args, cost=LIGHT):
    return pl.pallas_call(
        kernel,
        out_shape=shapes,
        in_specs=[SMEM] * smem + [VMEM] * (len(args) - smem),
        out_specs=[VMEM] * len(shapes),
        compiler_params=PARAMS,
        cost_estimate=cost,
        name=name,
    )(*args)


def label(parts):
    return "_".join(f"{h}{s}" for h, s in parts)


def prepare_call(order, where, q, g):
    shapes = [jax.ShapeDtypeStruct(s, bf16) for s in (
        (ROWS, WIDTH), (ROWS, KV_RANK), (WIDTH, ROWS), (KV_RANK, ROWS))]
    shapes += [jax.ShapeDtypeStruct((8 * PART, 128), jnp.int32), jax.ShapeDtypeStruct((8, ROWS), jnp.int32)]
    return call(prepare_kernel, "prepare", shapes, 2, [order, where, q, g])


def forward_call(parts, query_pos, key_pos, stat, keys, qt, gt):
    n = len(parts)
    counts = [len(k) for k in keys]
    rows = [r for k in keys for r in k]
    shapes = [jax.ShapeDtypeStruct((8, ROWS), f32)] + [jax.ShapeDtypeStruct((n * PART, ROWS), f32)] * 2

    def kernel(*refs):
        if stat is None:
            refs = (*refs[:2], None, *refs[2:])
        forward_kernel(parts, counts, *refs)

    args = [query_pos, key_pos] + ([] if stat is None else [stat]) + rows + [qt, gt]
    return call(kernel, "forward_" + label(parts), shapes, 0, args)


def backward_call(wanted, last, saved, taken, q, g):
    parts = [(saved[w][0], w[0] == 0) for w in wanted]
    shapes, args = [], [last]
    for w in wanted:
        shapes.append(jax.ShapeDtypeStruct((PART, SENT), f32 if w == (0, 0) else bf16))
        shapes.append(jax.ShapeDtypeStruct((PART, ROWS), bf16))
        args += list(saved[w][1:]) + ([] if w[0] else [taken[w[1]]])
    out = call(lambda *refs: backward_kernel(parts, *refs), "backward_" + label(wanted), shapes, 0, args + [q, g],
               LIGHT)
    return {w: (out[2 * i], out[2 * i + 1]) for i, w in enumerate(wanted)}


def query_call(pairs):
    counts = [len(k) for _, k in pairs]
    args = [a for ds, k in pairs for a in (ds, *k)]
    shapes = [jax.ShapeDtypeStruct((ROWS, WIDTH), bf16)]
    return call(lambda *refs: query_kernel(counts, *refs), "query_grad", shapes, 0, args)[0]


def shards(queries, latent, grad_out, block_order):
    tok_rows, head_count, width = queries.shape
    q = queries.reshape(tok_rows * head_count, width)
    g = grad_out.reshape(tok_rows * head_count, KV_RANK)
    where = jnp.stack([
        lax.axis_index(CTX), lax.axis_index("c"), lax.axis_index("x"),
        2 * lax.axis_index("yh") + lax.axis_index("yl"),
    ]).astype(jnp.int32)
    groups = first_groups()
    piece = lax.dynamic_slice_in_dim(latent, lax.axis_index(HEAD) * 8, 8, 0)
    piece = jnp.pad(piece, ((0, 0), (0, SENT - WIDTH)))
    first = lax.all_to_all(
        jnp.broadcast_to(piece[None], (32, 8, SENT)), ALL, 0, 0, axis_index_groups=groups, tiled=True
    ).reshape(PART, SENT)
    q, g, first = lax.optimization_barrier((q, g, first))
    keys = {(0, 0): [first]}
    keys[0, 1] = [turn(first, 1)]
    keys[0, 3] = [turn(first, 3)]
    q, g, qt, gt, key_pos, query_pos = prepare_call(block_order, where, q, g)
    stat = None
    saved = {}
    for wanted in FORWARD:
        for w in wanted:
            if w[0] == 0:
                if w[1] == 2:
                    keys[w] = [turn(keys[0, 1][0][:PART // 2], 1), turn(keys[0, 3][0][PART // 2:], 3)]
                if stat is not None:
                    (keys[w], stat) = lax.optimization_barrier((keys[w], stat))
                keys[1, w[1]] = [swap(k) for k in keys[w]]
        stat, p, vp = forward_call(wanted, query_pos, key_pos, stat, [keys[w] for w in wanted], qt, gt)
        for i, w in enumerate(wanted):
            saved[w] = (i, stat, p, vp)
    last = stat
    done = {}
    taken = {}
    arrived = []
    for wanted in BACKWARD:
        done.update(backward_call(wanted, last, saved, taken, q, g))
        for half, shift in wanted:
            if half:
                taken[shift] = swap(done[1, shift][0])
            elif shift:
                value, last = lax.optimization_barrier((done[0, shift][0], last))
                arrived.append(turn(value, 4 - shift))
    dq = query_call([(done[w][1], keys[w]) for w in ORDER])
    (arrived, dq) = lax.optimization_barrier((arrived, dq))
    arrived = [done[0, 0][0]] + [a.astype(f32) for a in arrived]
    part = (arrived[0] + arrived[1] + arrived[2] + arrived[3]).astype(bf16)
    part = lax.all_to_all(
        part.reshape(32, 8, SENT), ALL, 0, 0, axis_index_groups=groups, tiled=True
    )
    grad_latent = jnp.sum(part.astype(f32), axis=0)[:, :WIDTH]
    return dq.reshape(tok_rows, head_count, width), grad_latent


def solution(mesh):
    fine = Mesh(mesh.devices.reshape(SIZES), ALL)
    placed = (P(CTX, HEAD, None), P(CTX, None), P(CTX, HEAD, None), P())
    return jax.shard_map(
        shards, mesh=fine, in_specs=placed,
        out_specs=(P(CTX, HEAD, None), P(ALL, None)), check_vma=False,
    )
```

```python
import itertools

import jax
import jax.numpy as jnp
from jax import lax
from jax.experimental import pallas as pl
from jax.experimental.pallas import tpu as pltpu
from jax.sharding import Mesh, PartitionSpec as P

SIZES = (8, 2, 2, 2, 4)
CTX = ("z", "yl", "c")
HEAD = ("yh", "x")
ALL = CTX + HEAD
KV_RANK = 512
WIDTH = 576
SENT = 640
SCALE = 192.0 ** (-0.5)
LOW = -1e30
ROWS = 512
PART = 256
bf16, f32 = jnp.bfloat16, jnp.float32
FORWARD = (((0, 0),), ((0, 1), (0, 3)), ((0, 2), (1, 0), (1, 1), (1, 3)), ((1, 2),))
BACKWARD = (((1, 2, 0),), ((1, 1, 0), (1, 3, 0)), ((0, 2, 1), (0, 1, 0), (0, 3, 0)), ((1, 0, 0), (0, 0, 0)))
ORDER = tuple(w for call in FORWARD for w in call)


def places():
    return itertools.product(*(range(n) for n in SIZES))


def flat(z, yl, c, yh, x):
    return (((z * 2 + yl) * 2 + c) * 2 + yh) * 4 + x


def first_groups():
    found = {}
    for z, yl, c, yh, x in places():
        found.setdefault((c, x) if c == 0 else (c, yl, yh), []).append(flat(z, yl, c, yh, x))
    return list(found.values())


def turn(value, shift):
    pairs = []
    for z, yl, c, yh, x in places():
        y = 2 * yh + yl
        if c == 0:
            to = flat(z, yl, c, yh, (x + shift) % 4)
        else:
            y = (y + shift) % 4
            to = flat(z, y % 2, c, y // 2, x)
        pairs.append((flat(z, yl, c, yh, x), to))
    return lax.ppermute(value, ALL, pairs)


def swap(value):
    return lax.ppermute(value, "c", [(0, 1), (1, 0)])


def nn(a, b):
    return lax.dot_general(a, b, (((1,), (0,)), ((), ())), preferred_element_type=f32)


def tn(a, b):
    return lax.dot_general(a, b, (((0,), (0,)), ((), ())), preferred_element_type=f32)


def key_positions(order_ref, where_ref, key_core, shift):
    x = lax.rem(where_ref[2] + 4 - shift, 4)
    y = lax.rem(where_ref[3] + 4 - shift, 4)
    yl, yh = lax.rem(y, 2), y // 2
    sub = lax.broadcasted_iota(jnp.int32, (8, 128), 0)
    tiles = []
    for t in range(PART // 8):
        z, a, b = t // 4, (t // 2) % 2, t % 2
        first = ((z * 2 + a) * 2) * 2 + b
        second = ((z * 2 + yl) * 2 + 1) * 2 + yh
        block = jnp.where(key_core == 0, first, second)
        eighth = jnp.where(key_core == 0, x, t % 4)
        tiles.append(sub + (order_ref[block] * 32 + eighth * 8))
    return jnp.concatenate(tiles, axis=0)


def prepare_kernel(order_ref, where_ref, q_ref, g_ref, q_out, g_out, qt_out, gt_out, key_out, query_out):
    ctx, core = where_ref[0], where_ref[1]
    q, g = q_ref[...], g_ref[...]
    q_out[...] = q
    g_out[...] = g
    qt_out[...] = q.T
    gt_out[...] = g.T
    for i, (half, shift) in enumerate(ORDER):
        key_core = core if half == 0 else 1 - core
        key_out[i * PART:(i + 1) * PART, :] = key_positions(order_ref, where_ref, key_core, shift)
    tok = lax.broadcasted_iota(jnp.int32, (8, ROWS), 1) // 8
    query_out[...] = jnp.where(
        tok < 32, order_ref[2 * ctx] * 32 + tok, order_ref[2 * ctx + 1] * 32 + tok - 32
    )


def load_part(refs, width):
    rows = [r[:, :width] for r in refs]
    return rows[0] if len(rows) == 1 else jnp.concatenate(rows, axis=0)


def forward_kernel(parts, counts, *refs):
    query_pos_ref, key_pos_ref, stat_ref = refs[:3]
    key_refs, at = [], 3
    for count in counts:
        key_refs.append(refs[at:at + count])
        at += count
    qt_ref, gt_ref, stat_out, p_out, vp_out = refs[at:]
    query_pos = query_pos_ref[0:1, :]
    if stat_ref is None:
        running_max = jnp.full((1, ROWS), LOW, f32)
        total = weighted = jnp.zeros((1, ROWS), f32)
    else:
        running_max, total, weighted = stat_ref[0:1, :], stat_ref[1:2, :], stat_ref[2:3, :]
    qt, gt = qt_ref[...], gt_ref[...]
    for i, part in enumerate(parts):
        start = ORDER.index(part) * PART
        key_pos = key_pos_ref[start:start + PART, :]
        key_pos = jnp.concatenate([key_pos] * (ROWS // 128), axis=1)
        visible = key_pos <= query_pos
        scores = jnp.where(visible, nn(load_part(key_refs[i], WIDTH), qt) * SCALE, LOW)
        value_prod = nn(load_part(key_refs[i], KV_RANK), gt)
        new_max = jnp.maximum(running_max, jnp.max(scores, axis=0, keepdims=True))
        carry = jnp.exp(running_max - new_max)
        p = jnp.where(visible, jnp.exp(scores - new_max), 0.0)
        total = total * carry + jnp.sum(p, axis=0, keepdims=True)
        weighted = weighted * carry + jnp.sum(p * value_prod, axis=0, keepdims=True)
        running_max = new_max
        p_out[i * PART:(i + 1) * PART, :] = p
        vp_out[i * PART:(i + 1) * PART, :] = value_prod
        stat_out[3 + i:4 + i, :] = new_max
    stat_out[0:1, :] = running_max
    stat_out[1:2, :] = total
    stat_out[2:3, :] = weighted


def backward_kernel(parts, last_ref, *refs):
    at = sum(4 if added else 3 for _, added in parts)
    q, g = refs[at][...], refs[at + 1][...]
    outs = refs[at + 2:]
    inv = 1.0 / last_ref[1:2, :]
    delta = last_ref[2:3, :] * inv
    at = 0
    for i, (place, added) in enumerate(parts):
        stat_ref, p_ref, vp_ref = refs[at:at + 3]
        out_ref, ds_ref = outs[2 * i:2 * i + 2]
        rows = slice(place * PART, (place + 1) * PART)
        factor = jnp.exp(stat_ref[3 + place:4 + place, :] - last_ref[0:1, :]) * inv
        attention = p_ref[rows, :] * factor
        ds = (SCALE * attention * (vp_ref[rows, :] - delta)).astype(bf16)
        ds_ref[...] = ds
        term = nn(ds, q[:, :KV_RANK]) + nn(attention.astype(bf16), g)
        rope = nn(ds, q[:, KV_RANK:])
        if added:
            term = term + refs[at + 3][:, :KV_RANK].astype(f32)
            rope = rope + refs[at + 3][:, KV_RANK:WIDTH].astype(f32)
        out_ref[:, :KV_RANK] = term.astype(out_ref.dtype)
        out_ref[:, KV_RANK:] = jnp.concatenate([rope, jnp.zeros_like(rope)], axis=1).astype(out_ref.dtype)
        at += 4 if added else 3


def query_kernel(counts, *refs):
    out = refs[-1]
    ds, keys, at = [], [], 0
    for count in counts:
        ds.append(refs[at][...])
        keys.append(load_part(refs[at + 1:at + 1 + count], WIDTH))
        at += 1 + count
    out[...] = tn(jnp.concatenate(ds, axis=0), jnp.concatenate(keys, axis=0)).astype(bf16)


VMEM = pl.BlockSpec(memory_space=pltpu.VMEM)
SMEM = pl.BlockSpec(memory_space=pltpu.SMEM)
LIGHT = pl.CostEstimate(flops=1024, bytes_accessed=1024, transcendentals=0)
PARAMS = pltpu.CompilerParams(vmem_limit_bytes=20 * 2**20)


def call(kernel, name, shapes, smem, args, cost=LIGHT):
    return pl.pallas_call(
        kernel,
        out_shape=shapes,
        in_specs=[SMEM] * smem + [VMEM] * (len(args) - smem),
        out_specs=[VMEM] * len(shapes),
        compiler_params=PARAMS,
        cost_estimate=cost,
        name=name,
    )(*args)


def label(parts):
    return "_".join(f"{h}{s}" for h, s in parts)


def prepare_call(order, where, q, g):
    shapes = [jax.ShapeDtypeStruct(s, bf16) for s in (
        (ROWS, WIDTH), (ROWS, KV_RANK), (WIDTH, ROWS), (KV_RANK, ROWS))]
    shapes += [jax.ShapeDtypeStruct((8 * PART, 128), jnp.int32), jax.ShapeDtypeStruct((8, ROWS), jnp.int32)]
    return call(prepare_kernel, "prepare", shapes, 2, [order, where, q, g])


def forward_call(parts, query_pos, key_pos, stat, keys, qt, gt):
    n = len(parts)
    counts = [len(k) for k in keys]
    rows = [r for k in keys for r in k]
    shapes = [jax.ShapeDtypeStruct((8, ROWS), f32)] + [jax.ShapeDtypeStruct((n * PART, ROWS), f32)] * 2

    def kernel(*refs):
        if stat is None:
            refs = (*refs[:2], None, *refs[2:])
        forward_kernel(parts, counts, *refs)

    args = [query_pos, key_pos] + ([] if stat is None else [stat]) + rows + [qt, gt]
    return call(kernel, "forward_" + label(parts), shapes, 0, args)


def backward_call(wanted, last, saved, taken, q, g):
    parts = [(saved[h, s][0], added) for h, s, added in wanted]
    shapes, args = [], [last]
    for h, s, added in wanted:
        shapes.append(jax.ShapeDtypeStruct((PART, SENT), bf16 if h or added else f32))
        shapes.append(jax.ShapeDtypeStruct((PART, ROWS), bf16))
        args += list(saved[h, s][1:]) + ([taken[s]] if added else [])
    name = "backward_" + label([w[:2] for w in wanted])
    out = call(lambda *refs: backward_kernel(parts, *refs), name, shapes, 0, args + [q, g])
    return {w[:2]: (out[2 * i], out[2 * i + 1]) for i, w in enumerate(wanted)}


def add_kernel(*refs):
    n = len(refs) // 3
    for i in range(n):
        refs[2 * n + i][...] = (refs[i][...] + refs[n + i][...].astype(f32)).astype(bf16)


def add_call(kept, taken):
    shapes = [jax.ShapeDtypeStruct((PART, SENT), bf16)] * len(kept)
    return call(add_kernel, "add_cores", shapes, 0, [*kept, *taken])


def query_call(pairs):
    counts = [len(k) for _, k in pairs]
    args = [a for ds, k in pairs for a in (ds, *k)]
    shapes = [jax.ShapeDtypeStruct((ROWS, WIDTH), bf16)]
    return call(lambda *refs: query_kernel(counts, *refs), "query_grad", shapes, 0, args)[0]


def shards(queries, latent, grad_out, block_order):
    tok_rows, head_count, width = queries.shape
    q = queries.reshape(tok_rows * head_count, width)
    g = grad_out.reshape(tok_rows * head_count, KV_RANK)
    where = jnp.stack([
        lax.axis_index(CTX), lax.axis_index("c"), lax.axis_index("x"),
        2 * lax.axis_index("yh") + lax.axis_index("yl"),
    ]).astype(jnp.int32)
    groups = first_groups()
    piece = lax.dynamic_slice_in_dim(latent, lax.axis_index(HEAD) * 8, 8, 0)
    piece = jnp.pad(piece, ((0, 0), (0, SENT - WIDTH)))
    first = lax.all_to_all(
        jnp.broadcast_to(piece[None], (32, 8, SENT)), ALL, 0, 0, axis_index_groups=groups, tiled=True
    ).reshape(PART, SENT)
    q, g, first = lax.optimization_barrier((q, g, first))
    keys = {(0, 0): [first]}
    for shift in (1, 3, 2):
        keys[0, shift] = [turn(first, shift)]
    q, g, qt, gt, key_pos, query_pos = prepare_call(block_order, where, q, g)
    stat = None
    saved = {}
    for wanted in FORWARD:
        for w in wanted:
            if w[0] == 0:
                if stat is not None:
                    (keys[w], stat) = lax.optimization_barrier((keys[w], stat))
                keys[1, w[1]] = [swap(k) for k in keys[w]]
        stat, p, vp = forward_call(wanted, query_pos, key_pos, stat, [keys[w] for w in wanted], qt, gt)
        for i, w in enumerate(wanted):
            saved[w] = (i, stat, p, vp)
    last = stat
    done = {}
    taken = {}
    for wanted in BACKWARD[:3]:
        done.update(backward_call(wanted, last, saved, taken, q, g))
        for half, shift, _ in wanted:
            if half:
                taken[shift] = swap(done[1, shift][0])
    near = add_call([done[0, s][0] for s in (1, 3)], [taken[s] for s in (1, 3)])
    far, near, last = lax.optimization_barrier((done[0, 2][0], near, last))
    done.update(backward_call(BACKWARD[3], last, saved, taken, q, g))
    taken[0] = swap(done[1, 0][0])
    arrived = [turn(far, 2), turn(near[0], 3), turn(near[1], 1), taken[0]]
    dq = query_call([(done[w][1], keys[w]) for w in ORDER])
    (arrived, dq) = lax.optimization_barrier((arrived, dq))
    arrived = [a.astype(f32) for a in arrived] + [done[0, 0][0]]
    part = (arrived[0] + arrived[1] + arrived[2] + arrived[3] + arrived[4]).astype(bf16)
    part = lax.all_to_all(
        part.reshape(32, 8, SENT), ALL, 0, 0, axis_index_groups=groups, tiled=True
    )
    grad_latent = jnp.sum(part.astype(f32), axis=0)[:, :WIDTH]
    return dq.reshape(tok_rows, head_count, width), grad_latent


def solution(mesh):
    fine = Mesh(mesh.devices.reshape(SIZES), ALL)
    placed = (P(CTX, HEAD, None), P(CTX, None), P(CTX, HEAD, None), P())
    return jax.shard_map(
        shards, mesh=fine, in_specs=placed,
        out_specs=(P(CTX, HEAD, None), P(ALL, None)), check_vma=False,
    )
```

```python
import itertools

import jax
import jax.numpy as jnp
from jax import lax
from jax.experimental import pallas as pl
from jax.experimental.pallas import tpu as pltpu
from jax.sharding import Mesh, PartitionSpec as P

SIZES = (8, 2, 2, 2, 4)
CTX = ("z", "yl", "c")
HEAD = ("yh", "x")
ALL = CTX + HEAD
KV_RANK = 512
WIDTH = 576
SENT = 640
SCALE = 192.0 ** (-0.5)
LOW = -1e30
ROWS = 512
PART = 256
bf16, f32 = jnp.bfloat16, jnp.float32
FORWARD = (((0, 0),), ((0, 1), (0, 3), (1, 0)), ((0, 2), (1, 1), (1, 3)), ((1, 2),))
BACKWARD = (((1, 2, 0),), ((1, 1, 0), (1, 3, 0)), ((0, 2, 1), (0, 1, 0), (0, 3, 0)), ((1, 0, 0), (0, 0, 0)))
ORDER = tuple(w for call in FORWARD for w in call)


def places():
    return itertools.product(*(range(n) for n in SIZES))


def flat(z, yl, c, yh, x):
    return (((z * 2 + yl) * 2 + c) * 2 + yh) * 4 + x


def groups(key):
    found = {}
    for z, yl, c, yh, x in places():
        found.setdefault(key(z, yl, c, yh, x), []).append(flat(z, yl, c, yh, x))
    return list(found.values())


def gather_groups():
    return groups(lambda z, yl, c, yh, x: (c, yh, x) if c == 0 else (c, yl, yh, x // 2))


def scatter_groups():
    return groups(lambda z, yl, c, yh, x: (c, x) if c == 0 else (c, yl, yh))


def turn(value, shift):
    pairs = []
    for z, yl, c, yh, x in places():
        y = 2 * yh + yl
        if c == 0:
            to = flat(z, yl, c, yh, (x + shift) % 4)
        else:
            y = (y + shift) % 4
            to = flat(z, y % 2, c, y // 2, x)
        pairs.append((flat(z, yl, c, yh, x), to))
    return lax.ppermute(value, ALL, pairs)


def swap(value):
    return lax.ppermute(value, "c", [(0, 1), (1, 0)])


def nn(a, b):
    return lax.dot_general(a, b, (((1,), (0,)), ((), ())), preferred_element_type=f32)


def tn(a, b):
    return lax.dot_general(a, b, (((0,), (0,)), ((), ())), preferred_element_type=f32)


def key_positions(order_ref, where_ref, key_core, shift):
    x = lax.rem(where_ref[2] + 4 - shift, 4)
    y = lax.rem(where_ref[3] + 4 - shift, 4)
    yl, yh = lax.rem(y, 2), y // 2
    sub = lax.broadcasted_iota(jnp.int32, (8, 128), 0)
    tiles = []
    for t in range(PART // 8):
        z, a, b = t // 4, (t // 2) % 2, t % 2
        first = ((z * 2 + a) * 2) * 2 + b
        second = ((z * 2 + yl) * 2 + 1) * 2 + yh
        block = jnp.where(key_core == 0, first, second)
        eighth = jnp.where(key_core == 0, x, t % 4)
        tiles.append(sub + (order_ref[block] * 32 + eighth * 8))
    return jnp.concatenate(tiles, axis=0)


def prepare_kernel(where_ref, order_hbm, q_hbm, g_hbm, q_out, g_out, qt_out, gt_out, key_out, query_out,
                   order_ref, sems):
    copies = [
        pltpu.make_async_copy(order_hbm, order_ref, sems.at[0]),
        pltpu.make_async_copy(q_hbm, q_out, sems.at[1]),
        pltpu.make_async_copy(g_hbm, g_out, sems.at[2]),
    ]
    for copy in copies:
        copy.start()
    ctx, core = where_ref[0], where_ref[1]
    copies[0].wait()
    for i, (half, shift) in enumerate(ORDER):
        key_core = core if half == 0 else 1 - core
        key_out[i * PART:(i + 1) * PART, :] = key_positions(order_ref, where_ref, key_core, shift)
    tok = lax.broadcasted_iota(jnp.int32, (8, ROWS), 1) // 8
    query_out[...] = jnp.where(
        tok < 32, order_ref[2 * ctx] * 32 + tok, order_ref[2 * ctx + 1] * 32 + tok - 32
    )
    copies[1].wait()
    qt_out[...] = q_out[...].T
    copies[2].wait()
    gt_out[...] = g_out[...].T


def load_part(refs, width):
    rows = [r[:, :width] for r in refs]
    return rows[0] if len(rows) == 1 else jnp.concatenate(rows, axis=0)


def forward_kernel(parts, counts, *refs):
    query_pos_ref, key_pos_ref, stat_ref = refs[:3]
    key_refs, at = [], 3
    for count in counts:
        key_refs.append(refs[at:at + count])
        at += count
    qt_ref, gt_ref, stat_out, p_out, vp_out = refs[at:]
    query_pos = query_pos_ref[0:1, :]
    if stat_ref is None:
        running_max = jnp.full((1, ROWS), LOW, f32)
        total = weighted = jnp.zeros((1, ROWS), f32)
    else:
        running_max, total, weighted = stat_ref[0:1, :], stat_ref[1:2, :], stat_ref[2:3, :]
    qt, gt = qt_ref[...], gt_ref[...]
    for i, part in enumerate(parts):
        start = ORDER.index(part) * PART
        key_pos = key_pos_ref[start:start + PART, :]
        key_pos = jnp.concatenate([key_pos] * (ROWS // 128), axis=1)
        visible = key_pos <= query_pos
        scores = jnp.where(visible, nn(load_part(key_refs[i], WIDTH), qt) * SCALE, LOW)
        value_prod = nn(load_part(key_refs[i], KV_RANK), gt)
        new_max = jnp.maximum(running_max, jnp.max(scores, axis=0, keepdims=True))
        carry = jnp.exp(running_max - new_max)
        p = jnp.where(visible, jnp.exp(scores - new_max), 0.0)
        total = total * carry + jnp.sum(p, axis=0, keepdims=True)
        weighted = weighted * carry + jnp.sum(p * value_prod, axis=0, keepdims=True)
        running_max = new_max
        p_out[i * PART:(i + 1) * PART, :] = p
        vp_out[i * PART:(i + 1) * PART, :] = value_prod
        stat_out[3 + i:4 + i, :] = new_max
    stat_out[0:1, :] = running_max
    stat_out[1:2, :] = total
    stat_out[2:3, :] = weighted


def backward_kernel(parts, last_ref, *refs):
    at = sum(4 if added else 3 for _, added in parts)
    q, g = refs[at][...], refs[at + 1][...]
    outs = refs[at + 2:]
    inv = 1.0 / last_ref[1:2, :]
    delta = last_ref[2:3, :] * inv
    at = 0
    for i, (place, added) in enumerate(parts):
        stat_ref, p_ref, vp_ref = refs[at:at + 3]
        out_ref, ds_ref = outs[2 * i:2 * i + 2]
        rows = slice(place * PART, (place + 1) * PART)
        factor = jnp.exp(stat_ref[3 + place:4 + place, :] - last_ref[0:1, :]) * inv
        attention = p_ref[rows, :] * factor
        ds = (SCALE * attention * (vp_ref[rows, :] - delta)).astype(bf16)
        ds_ref[...] = ds
        term = nn(ds, q[:, :KV_RANK]) + nn(attention.astype(bf16), g)
        rope = nn(ds, q[:, KV_RANK:])
        if added:
            term = term + refs[at + 3][:, :KV_RANK].astype(f32)
            rope = rope + refs[at + 3][:, KV_RANK:WIDTH].astype(f32)
        out_ref[:, :KV_RANK] = term.astype(out_ref.dtype)
        out_ref[:, KV_RANK:] = jnp.concatenate([rope, jnp.zeros_like(rope)], axis=1).astype(out_ref.dtype)
        at += 4 if added else 3


def query_kernel(counts, *refs):
    out = refs[-1]
    ds, keys, at = [], [], 0
    for count in counts:
        ds.append(refs[at][...])
        keys.append(load_part(refs[at + 1:at + 1 + count], WIDTH))
        at += 1 + count
    out[...] = tn(jnp.concatenate(ds, axis=0), jnp.concatenate(keys, axis=0)).astype(bf16)


VMEM = pl.BlockSpec(memory_space=pltpu.VMEM)
SMEM = pl.BlockSpec(memory_space=pltpu.SMEM)
LIGHT = pl.CostEstimate(flops=1024, bytes_accessed=1024, transcendentals=0)
PARAMS = pltpu.CompilerParams(vmem_limit_bytes=20 * 2**20)


def call(kernel, name, shapes, smem, args, cost=LIGHT):
    return pl.pallas_call(
        kernel,
        out_shape=shapes,
        in_specs=[SMEM] * smem + [VMEM] * (len(args) - smem),
        out_specs=[VMEM] * len(shapes),
        compiler_params=PARAMS,
        cost_estimate=cost,
        name=name,
    )(*args)


def label(parts):
    return "_".join(f"{h}{s}" for h, s in parts)


def prepare_call(order, where, q, g):
    shapes = [jax.ShapeDtypeStruct(s, bf16) for s in (
        (ROWS, WIDTH), (ROWS, KV_RANK), (WIDTH, ROWS), (KV_RANK, ROWS))]
    shapes += [jax.ShapeDtypeStruct((8 * PART, 128), jnp.int32), jax.ShapeDtypeStruct((8, ROWS), jnp.int32)]
    return pl.pallas_call(
        prepare_kernel,
        out_shape=shapes,
        in_specs=[SMEM] + [pl.BlockSpec(memory_space=pltpu.HBM)] * 3,
        out_specs=[VMEM] * len(shapes),
        scratch_shapes=[pltpu.SMEM((64,), jnp.int32), pltpu.SemaphoreType.DMA((3,))],
        compiler_params=PARAMS,
        cost_estimate=LIGHT,
        name="prepare",
    )(where, order, q, g)


def forward_call(parts, query_pos, key_pos, stat, keys, qt, gt):
    n = len(parts)
    counts = [len(k) for k in keys]
    rows = [r for k in keys for r in k]
    shapes = [jax.ShapeDtypeStruct((8, ROWS), f32)] + [jax.ShapeDtypeStruct((n * PART, ROWS), f32)] * 2

    def kernel(*refs):
        if stat is None:
            refs = (*refs[:2], None, *refs[2:])
        forward_kernel(parts, counts, *refs)

    args = [query_pos, key_pos] + ([] if stat is None else [stat]) + rows + [qt, gt]
    return call(kernel, "forward_" + label(parts), shapes, 0, args)


def backward_call(wanted, last, saved, taken, q, g):
    parts = [(saved[h, s][0], added) for h, s, added in wanted]
    shapes, args = [], [last]
    for h, s, added in wanted:
        shapes.append(jax.ShapeDtypeStruct((PART, SENT), bf16 if h or added else f32))
        shapes.append(jax.ShapeDtypeStruct((PART, ROWS), bf16))
        args += list(saved[h, s][1:]) + ([taken[s]] if added else [])
    name = "backward_" + label([w[:2] for w in wanted])
    out = call(lambda *refs: backward_kernel(parts, *refs), name, shapes, 0, args + [q, g])
    return {w[:2]: (out[2 * i], out[2 * i + 1]) for i, w in enumerate(wanted)}


def add_kernel(*refs):
    n = len(refs) // 3
    for i in range(n):
        refs[2 * n + i][...] = (refs[i][...] + refs[n + i][...].astype(f32)).astype(bf16)


def add_call(kept, taken):
    shapes = [jax.ShapeDtypeStruct((PART, SENT), bf16)] * len(kept)
    return call(add_kernel, "add_cores", shapes, 0, [*kept, *taken])


def query_call(pairs):
    counts = [len(k) for _, k in pairs]
    args = [a for ds, k in pairs for a in (ds, *k)]
    shapes = [jax.ShapeDtypeStruct((ROWS, WIDTH), bf16)]
    return call(lambda *refs: query_kernel(counts, *refs), "query_grad", shapes, 0, args)[0]


def shards(queries, latent, grad_out, block_order):
    tok_rows, head_count, width = queries.shape
    q = queries.reshape(tok_rows * head_count, width)
    g = grad_out.reshape(tok_rows * head_count, KV_RANK)
    where = jnp.stack([
        lax.axis_index(CTX), lax.axis_index("c"), lax.axis_index("x"),
        2 * lax.axis_index("yh") + lax.axis_index("yl"),
    ]).astype(jnp.int32)
    core, x, yh = lax.axis_index("c"), lax.axis_index("x"), lax.axis_index("yh")
    low = jnp.where(core == 0, x, yh * 4 + 2 * (x % 2)) * 8
    high = jnp.where(core == 0, x + 4, yh * 4 + 2 * (x % 2) + 1) * 8
    piece = jnp.concatenate([lax.dynamic_slice_in_dim(latent, at, 8, 0) for at in (low, high)])
    piece = jnp.pad(piece, ((0, 0), (0, SENT - WIDTH)))
    first = lax.all_to_all(
        jnp.broadcast_to(piece[None], (16, 16, SENT)), ALL, 0, 0,
        axis_index_groups=gather_groups(), tiled=True,
    ).reshape(PART, SENT)
    q, g, first = lax.optimization_barrier((q, g, first))
    keys = {(0, 0): [first]}
    for shift in (2, 1, 3):
        keys[0, shift] = [turn(first, shift)]
    q, g, qt, gt, key_pos, query_pos = prepare_call(block_order, where, q, g)
    stat = None
    saved = {}
    for wanted in FORWARD:
        for w in wanted:
            if w[0] == 0:
                if stat is not None:
                    (keys[w], stat) = lax.optimization_barrier((keys[w], stat))
                keys[1, w[1]] = [swap(k) for k in keys[w]]
        stat, p, vp = forward_call(wanted, query_pos, key_pos, stat, [keys[w] for w in wanted], qt, gt)
        for i, w in enumerate(wanted):
            saved[w] = (i, stat, p, vp)
    last = stat
    done = {}
    taken = {}
    for wanted in BACKWARD[:3]:
        done.update(backward_call(wanted, last, saved, taken, q, g))
        for half, shift, _ in wanted:
            if half:
                taken[shift] = swap(done[1, shift][0])
    near = add_call([done[0, s][0] for s in (1, 3)], [taken[s] for s in (1, 3)])
    far, near, last = lax.optimization_barrier((done[0, 2][0], near, last))
    done.update(backward_call(BACKWARD[3], last, saved, taken, q, g))
    taken[0] = swap(done[1, 0][0])
    arrived = [turn(far, 2), turn(near[0], 3), turn(near[1], 1), taken[0]]
    dq = query_call([(done[w][1], keys[w]) for w in ORDER])
    (arrived, dq) = lax.optimization_barrier((arrived, dq))
    arrived = [a.astype(f32) for a in arrived] + [done[0, 0][0]]
    part = (arrived[0] + arrived[1] + arrived[2] + arrived[3] + arrived[4]).astype(bf16)
    part = lax.all_to_all(
        part.reshape(32, 8, SENT), ALL, 0, 0, axis_index_groups=scatter_groups(), tiled=True
    )
    grad_latent = jnp.sum(part.astype(f32), axis=0)[:, :WIDTH]
    return dq.reshape(tok_rows, head_count, width), grad_latent


def solution(mesh):
    fine = Mesh(mesh.devices.reshape(SIZES), ALL)
    placed = (P(CTX, HEAD, None), P(CTX, None), P(CTX, HEAD, None), P())
    return jax.shard_map(
        shards, mesh=fine, in_specs=placed,
        out_specs=(P(CTX, HEAD, None), P(ALL, None)), check_vma=False,
    )
```

```python
import itertools

import jax
import jax.numpy as jnp
from jax import lax
from jax.experimental import pallas as pl
from jax.experimental.pallas import tpu as pltpu
from jax.sharding import Mesh, PartitionSpec as P

SIZES = (8, 2, 2, 2, 4)
CTX = ("z", "yl", "c")
HEAD = ("yh", "x")
ALL = CTX + HEAD
KV_RANK = 512
WIDTH = 576
SENT = 640
SCALE = 192.0 ** (-0.5)
LOW = -1e30
ROWS = 512
PART = 256
bf16, f32 = jnp.bfloat16, jnp.float32
FORWARD = (((0, 0),), ((0, 1), (0, 3), (1, 0)), ((0, 2), (1, 1), (1, 3)))
LAST = (1, 2)
BACKWARD = (((1, 1, 0), (1, 3, 0)), ((0, 2, 1), (0, 1, 0), (0, 3, 0)), ((1, 0, 0), (0, 0, 0)))
ORDER = tuple(w for call in FORWARD for w in call) + (LAST,)


def places():
    return itertools.product(*(range(n) for n in SIZES))


def flat(z, yl, c, yh, x):
    return (((z * 2 + yl) * 2 + c) * 2 + yh) * 4 + x


def groups(key):
    found = {}
    for z, yl, c, yh, x in places():
        found.setdefault(key(z, yl, c, yh, x), []).append(flat(z, yl, c, yh, x))
    return list(found.values())


def gather_groups():
    return groups(lambda z, yl, c, yh, x: (c, yh, x) if c == 0 else (c, yl, yh, x // 2))


def scatter_groups():
    return groups(lambda z, yl, c, yh, x: (c, x) if c == 0 else (c, yl, yh))


def turn(value, shift):
    pairs = []
    for z, yl, c, yh, x in places():
        y = 2 * yh + yl
        if c == 0:
            to = flat(z, yl, c, yh, (x + shift) % 4)
        else:
            y = (y + shift) % 4
            to = flat(z, y % 2, c, y // 2, x)
        pairs.append((flat(z, yl, c, yh, x), to))
    return lax.ppermute(value, ALL, pairs)


def swap(value):
    return lax.ppermute(value, "c", [(0, 1), (1, 0)])


def nn(a, b):
    return lax.dot_general(a, b, (((1,), (0,)), ((), ())), preferred_element_type=f32)


def tn(a, b):
    return lax.dot_general(a, b, (((0,), (0,)), ((), ())), preferred_element_type=f32)


def key_positions(order_ref, where_ref, key_core, shift):
    x = lax.rem(where_ref[2] + 4 - shift, 4)
    y = lax.rem(where_ref[3] + 4 - shift, 4)
    yl, yh = lax.rem(y, 2), y // 2
    sub = lax.broadcasted_iota(jnp.int32, (8, 128), 0)
    tiles = []
    for t in range(PART // 8):
        z, a, b = t // 4, (t // 2) % 2, t % 2
        first = ((z * 2 + a) * 2) * 2 + b
        second = ((z * 2 + yl) * 2 + 1) * 2 + yh
        block = jnp.where(key_core == 0, first, second)
        eighth = jnp.where(key_core == 0, x, t % 4)
        tiles.append(sub + (order_ref[block] * 32 + eighth * 8))
    return jnp.concatenate(tiles, axis=0)


def prepare_kernel(where_ref, order_hbm, q_hbm, g_hbm, q_out, g_out, qt_out, gt_out, key_out, query_out,
                   order_ref, sems):
    copies = [
        pltpu.make_async_copy(order_hbm, order_ref, sems.at[0]),
        pltpu.make_async_copy(q_hbm, q_out, sems.at[1]),
        pltpu.make_async_copy(g_hbm, g_out, sems.at[2]),
    ]
    for copy in copies:
        copy.start()
    ctx, core = where_ref[0], where_ref[1]
    copies[0].wait()
    for i, (half, shift) in enumerate(ORDER):
        key_core = core if half == 0 else 1 - core
        key_out[i * PART:(i + 1) * PART, :] = key_positions(order_ref, where_ref, key_core, shift)
    tok = lax.broadcasted_iota(jnp.int32, (8, ROWS), 1) // 8
    query_out[...] = jnp.where(
        tok < 32, order_ref[2 * ctx] * 32 + tok, order_ref[2 * ctx + 1] * 32 + tok - 32
    )
    copies[1].wait()
    qt_out[...] = q_out[...].T
    copies[2].wait()
    gt_out[...] = g_out[...].T


def load_part(refs, width):
    rows = [r[:, :width] for r in refs]
    return rows[0] if len(rows) == 1 else jnp.concatenate(rows, axis=0)


def forward_kernel(parts, counts, *refs):
    query_pos_ref, key_pos_ref, stat_ref = refs[:3]
    key_refs, at = [], 3
    for count in counts:
        key_refs.append(refs[at:at + count])
        at += count
    qt_ref, gt_ref, stat_out, p_out, vp_out = refs[at:]
    query_pos = query_pos_ref[0:1, :]
    if stat_ref is None:
        running_max = jnp.full((1, ROWS), LOW, f32)
        total = weighted = jnp.zeros((1, ROWS), f32)
    else:
        running_max, total, weighted = stat_ref[0:1, :], stat_ref[1:2, :], stat_ref[2:3, :]
    qt, gt = qt_ref[...], gt_ref[...]
    for i, part in enumerate(parts):
        start = ORDER.index(part) * PART
        key_pos = key_pos_ref[start:start + PART, :]
        key_pos = jnp.concatenate([key_pos] * (ROWS // 128), axis=1)
        visible = key_pos <= query_pos
        scores = jnp.where(visible, nn(load_part(key_refs[i], WIDTH), qt) * SCALE, LOW)
        value_prod = nn(load_part(key_refs[i], KV_RANK), gt)
        new_max = jnp.maximum(running_max, jnp.max(scores, axis=0, keepdims=True))
        carry = jnp.exp(running_max - new_max)
        p = jnp.where(visible, jnp.exp(scores - new_max), 0.0)
        total = total * carry + jnp.sum(p, axis=0, keepdims=True)
        weighted = weighted * carry + jnp.sum(p * value_prod, axis=0, keepdims=True)
        running_max = new_max
        p_out[i * PART:(i + 1) * PART, :] = p
        vp_out[i * PART:(i + 1) * PART, :] = value_prod
        stat_out[3 + i:4 + i, :] = new_max
    stat_out[0:1, :] = running_max
    stat_out[1:2, :] = total
    stat_out[2:3, :] = weighted


def backward_kernel(parts, last_ref, *refs):
    at = sum(4 if added else 3 for _, added in parts)
    q, g = refs[at][...], refs[at + 1][...]
    outs = refs[at + 2:]
    inv = 1.0 / last_ref[1:2, :]
    delta = last_ref[2:3, :] * inv
    at = 0
    for i, (place, added) in enumerate(parts):
        stat_ref, p_ref, vp_ref = refs[at:at + 3]
        out_ref, ds_ref = outs[2 * i:2 * i + 2]
        rows = slice(place * PART, (place + 1) * PART)
        factor = jnp.exp(stat_ref[3 + place:4 + place, :] - last_ref[0:1, :]) * inv
        attention = p_ref[rows, :] * factor
        ds = (SCALE * attention * (vp_ref[rows, :] - delta)).astype(bf16)
        ds_ref[...] = ds
        term = nn(ds, q[:, :KV_RANK]) + nn(attention.astype(bf16), g)
        rope = nn(ds, q[:, KV_RANK:])
        if added:
            term = term + refs[at + 3][:, :KV_RANK].astype(f32)
            rope = rope + refs[at + 3][:, KV_RANK:WIDTH].astype(f32)
        out_ref[:, :KV_RANK] = term.astype(out_ref.dtype)
        out_ref[:, KV_RANK:] = jnp.concatenate([rope, jnp.zeros_like(rope)], axis=1).astype(out_ref.dtype)
        at += 4 if added else 3


def turning_kernel(part, query_pos_ref, key_pos_ref, stat_ref, key_ref, qt_ref, gt_ref, q_ref, g_ref,
                   stat_out, out_ref, ds_ref):
    start = ORDER.index(part) * PART
    key_pos = key_pos_ref[start:start + PART, :]
    key_pos = jnp.concatenate([key_pos] * (ROWS // 128), axis=1)
    visible = key_pos <= query_pos_ref[0:1, :]
    scores = jnp.where(visible, nn(key_ref[:, :WIDTH], qt_ref[...]) * SCALE, LOW)
    value_prod = nn(key_ref[:, :KV_RANK], gt_ref[...])
    final_max = jnp.maximum(stat_ref[0:1, :], jnp.max(scores, axis=0, keepdims=True))
    carry = jnp.exp(stat_ref[0:1, :] - final_max)
    p = jnp.where(visible, jnp.exp(scores - final_max), 0.0)
    total = stat_ref[1:2, :] * carry + jnp.sum(p, axis=0, keepdims=True)
    weighted = stat_ref[2:3, :] * carry + jnp.sum(p * value_prod, axis=0, keepdims=True)
    stat_out[0:1, :] = final_max
    stat_out[1:2, :] = total
    stat_out[2:3, :] = weighted
    inv = 1.0 / total
    attention = p * inv
    ds = (SCALE * attention * (value_prod - weighted * inv)).astype(bf16)
    ds_ref[...] = ds
    q = q_ref[...]
    out_ref[:, :KV_RANK] = (nn(ds, q[:, :KV_RANK]) + nn(attention.astype(bf16), g_ref[...])).astype(bf16)
    rope = nn(ds, q[:, KV_RANK:])
    out_ref[:, KV_RANK:] = jnp.concatenate([rope, jnp.zeros_like(rope)], axis=1).astype(bf16)


def turning_call(part, query_pos, key_pos, stat, keys, qt, gt, q, g):
    shapes = [
        jax.ShapeDtypeStruct((8, ROWS), f32), jax.ShapeDtypeStruct((PART, SENT), bf16),
        jax.ShapeDtypeStruct((PART, ROWS), bf16),
    ]
    args = [query_pos, key_pos, stat, *keys, qt, gt, q, g]
    return call(lambda *refs: turning_kernel(part, *refs), "turning_" + label([part]), shapes, 0, args)


def query_kernel(counts, *refs):
    out = refs[-1]
    ds, keys, at = [], [], 0
    for count in counts:
        ds.append(refs[at][...])
        keys.append(load_part(refs[at + 1:at + 1 + count], WIDTH))
        at += 1 + count
    out[...] = tn(jnp.concatenate(ds, axis=0), jnp.concatenate(keys, axis=0)).astype(bf16)


VMEM = pl.BlockSpec(memory_space=pltpu.VMEM)
SMEM = pl.BlockSpec(memory_space=pltpu.SMEM)
LIGHT = pl.CostEstimate(flops=1024, bytes_accessed=1024, transcendentals=0)
PARAMS = pltpu.CompilerParams(vmem_limit_bytes=20 * 2**20)


def call(kernel, name, shapes, smem, args, cost=LIGHT):
    return pl.pallas_call(
        kernel,
        out_shape=shapes,
        in_specs=[SMEM] * smem + [VMEM] * (len(args) - smem),
        out_specs=[VMEM] * len(shapes),
        compiler_params=PARAMS,
        cost_estimate=cost,
        name=name,
    )(*args)


def label(parts):
    return "_".join(f"{h}{s}" for h, s in parts)


def prepare_call(order, where, q, g):
    shapes = [jax.ShapeDtypeStruct(s, bf16) for s in (
        (ROWS, WIDTH), (ROWS, KV_RANK), (WIDTH, ROWS), (KV_RANK, ROWS))]
    shapes += [jax.ShapeDtypeStruct((8 * PART, 128), jnp.int32), jax.ShapeDtypeStruct((8, ROWS), jnp.int32)]
    return pl.pallas_call(
        prepare_kernel,
        out_shape=shapes,
        in_specs=[SMEM] + [pl.BlockSpec(memory_space=pltpu.HBM)] * 3,
        out_specs=[VMEM] * len(shapes),
        scratch_shapes=[pltpu.SMEM((64,), jnp.int32), pltpu.SemaphoreType.DMA((3,))],
        compiler_params=PARAMS,
        cost_estimate=LIGHT,
        name="prepare",
    )(where, order, q, g)


def forward_call(parts, query_pos, key_pos, stat, keys, qt, gt):
    n = len(parts)
    counts = [len(k) for k in keys]
    rows = [r for k in keys for r in k]
    shapes = [jax.ShapeDtypeStruct((8, ROWS), f32)] + [jax.ShapeDtypeStruct((n * PART, ROWS), f32)] * 2

    def kernel(*refs):
        if stat is None:
            refs = (*refs[:2], None, *refs[2:])
        forward_kernel(parts, counts, *refs)

    args = [query_pos, key_pos] + ([] if stat is None else [stat]) + rows + [qt, gt]
    return call(kernel, "forward_" + label(parts), shapes, 0, args)


def backward_call(wanted, last, saved, taken, q, g):
    parts = [(saved[h, s][0], added) for h, s, added in wanted]
    shapes, args = [], [last]
    for h, s, added in wanted:
        shapes.append(jax.ShapeDtypeStruct((PART, SENT), bf16 if h or added else f32))
        shapes.append(jax.ShapeDtypeStruct((PART, ROWS), bf16))
        args += list(saved[h, s][1:]) + ([taken[s]] if added else [])
    name = "backward_" + label([w[:2] for w in wanted])
    out = call(lambda *refs: backward_kernel(parts, *refs), name, shapes, 0, args + [q, g])
    return {w[:2]: (out[2 * i], out[2 * i + 1]) for i, w in enumerate(wanted)}


def add_kernel(*refs):
    n = len(refs) // 3
    for i in range(n):
        refs[2 * n + i][...] = (refs[i][...] + refs[n + i][...].astype(f32)).astype(bf16)


def add_call(kept, taken):
    shapes = [jax.ShapeDtypeStruct((PART, SENT), bf16)] * len(kept)
    return call(add_kernel, "add_cores", shapes, 0, [*kept, *taken])


def query_call(pairs):
    counts = [len(k) for _, k in pairs]
    args = [a for ds, k in pairs for a in (ds, *k)]
    shapes = [jax.ShapeDtypeStruct((ROWS, WIDTH), bf16)]
    return call(lambda *refs: query_kernel(counts, *refs), "query_grad", shapes, 0, args)[0]


def shards(queries, latent, grad_out, block_order):
    tok_rows, head_count, width = queries.shape
    q = queries.reshape(tok_rows * head_count, width)
    g = grad_out.reshape(tok_rows * head_count, KV_RANK)
    where = jnp.stack([
        lax.axis_index(CTX), lax.axis_index("c"), lax.axis_index("x"),
        2 * lax.axis_index("yh") + lax.axis_index("yl"),
    ]).astype(jnp.int32)
    core, x, yh = lax.axis_index("c"), lax.axis_index("x"), lax.axis_index("yh")
    low = jnp.where(core == 0, x, yh * 4 + 2 * (x % 2)) * 8
    high = jnp.where(core == 0, x + 4, yh * 4 + 2 * (x % 2) + 1) * 8
    piece = jnp.concatenate([lax.dynamic_slice_in_dim(latent, at, 8, 0) for at in (low, high)])
    piece = jnp.pad(piece, ((0, 0), (0, SENT - WIDTH)))
    first = lax.all_to_all(
        jnp.broadcast_to(piece[None], (16, 16, SENT)), ALL, 0, 0,
        axis_index_groups=gather_groups(), tiled=True,
    ).reshape(PART, SENT)
    q, g, first = lax.optimization_barrier((q, g, first))
    keys = {(0, 0): [first]}
    for shift in (2, 1, 3):
        keys[0, shift] = [turn(first, shift)]
    q, g, qt, gt, key_pos, query_pos = prepare_call(block_order, where, q, g)
    stat = None
    saved = {}
    for wanted in FORWARD:
        for w in wanted:
            if w[0] == 0:
                if stat is not None:
                    (keys[w], stat) = lax.optimization_barrier((keys[w], stat))
                keys[1, w[1]] = [swap(k) for k in keys[w]]
        stat, p, vp = forward_call(wanted, query_pos, key_pos, stat, [keys[w] for w in wanted], qt, gt)
        for i, w in enumerate(wanted):
            saved[w] = (i, stat, p, vp)
    last, *turned = turning_call(LAST, query_pos, key_pos, stat, keys[LAST], qt, gt, q, g)
    done = {LAST: tuple(turned)}
    taken = {LAST[1]: swap(turned[0])}
    for wanted in BACKWARD[:2]:
        done.update(backward_call(wanted, last, saved, taken, q, g))
        for half, shift, _ in wanted:
            if half:
                taken[shift] = swap(done[1, shift][0])
    near = add_call([done[0, s][0] for s in (1, 3)], [taken[s] for s in (1, 3)])
    far, near, last = lax.optimization_barrier((done[0, 2][0], near, last))
    done.update(backward_call(BACKWARD[2], last, saved, taken, q, g))
    taken[0] = swap(done[1, 0][0])
    arrived = [turn(far, 2), turn(near[0], 3), turn(near[1], 1), taken[0]]
    dq = query_call([(done[w][1], keys[w]) for w in ORDER])
    (arrived, dq) = lax.optimization_barrier((arrived, dq))
    arrived = [a.astype(f32) for a in arrived] + [done[0, 0][0]]
    part = (arrived[0] + arrived[1] + arrived[2] + arrived[3] + arrived[4]).astype(bf16)
    part = lax.all_to_all(
        part.reshape(32, 8, SENT), ALL, 0, 0, axis_index_groups=scatter_groups(), tiled=True
    )
    grad_latent = jnp.sum(part.astype(f32), axis=0)[:, :WIDTH]
    return dq.reshape(tok_rows, head_count, width), grad_latent


def solution(mesh):
    fine = Mesh(mesh.devices.reshape(SIZES), ALL)
    placed = (P(CTX, HEAD, None), P(CTX, None), P(CTX, HEAD, None), P())
    return jax.shard_map(
        shards, mesh=fine, in_specs=placed,
        out_specs=(P(CTX, HEAD, None), P(ALL, None)), check_vma=False,
    )
```
